32 devices in a mesh: gx: 4 (over y, x), gy: 8 (over z, core).
Axes of the slice: x: 2, y: 2, z: 4, core: 2. Of those that a mesh axis runs over, the one named last changes fastest.
Arguments:
- particles: float32 [4, 8, 32, 6, 128], P('gx', 'gy'), may hold values from -5 to 5, as said below
- dinv: float32 [4, 8, 32, 128, 128], P('gx', 'gy'), may hold values from -2 to 2
- low_bound: float32 [1], replicated, may hold values from 0.3 to 0.6
- high_bound: float32 [1], replicated, may hold values from 2.2 to 3.2
- counts: int32 [4, 8], P('gx', 'gy'), may hold values from 24 to 32, as said below
- send_list: int32 [4, 8, 24], P('gx', 'gy'), may hold values from 0 to 31, as said below
- nbr_dir: int32 [4, 8, 32, 9], P('gx', 'gy'), may hold values from 0 to 8, as said below
- nbr_slot: int32 [4, 8, 32, 9], P('gx', 'gy'), may hold values from 0 to 31, as said below
Outputs:
- pressure: float32 [4, 8, 32, 128], P('gx', 'gy')
- velocity: float32 [4, 8, 32, 3, 128], P('gx', 'gy')
The draws below stay inside these ranges and needn't reach their ends.
Inputs may be any that keep to these rules, and one draw needn't show every extreme that they name: `counts`: device (0, 0) has all 32 slots live; live tiles fill the lowest slots. `send_list`: 24 distinct live slots of the device. `nbr_dir`: entry 0 of every tile is 4 (its own device). Other codes name only devices that exist. `nbr_slot`: entry 0 is the tile's own slot. For code 4 other entries are live slots of the device; for other codes, positions below 24 in the owner's send_list. `particles`: positions lie in [0, 1).
All inputs are finite; a program needn't handle non-finite values.
Results may differ from the reference program's by a relative error of at most 0.0003.
Values sent between devices are 32-bit elements; how exact they have to be, the bound alone decides.
A program may use at most 128 MiB of HBM per device.

```python
import math
import jax
import jax.numpy as jnp
from jax import lax

TILE = 128
K = 9
ITERS = 3
S = 32
G = 24
PX = 4
PY = 8


def layout(key):
    keys = jax.random.split(key, 6)
    counts = jax.random.randint(keys[0], (PX, PY), G, S + 1).astype(jnp.int32)
    counts = counts.at[0, 0].set(S)
    slot_iota = lax.broadcasted_iota(jnp.int32, (PX, PY, S), 2)
    active_flags = slot_iota < counts[:, :, None]
    score = jax.random.randint(keys[1], (PX, PY, S), 0, 1 << 16).astype(jnp.int32) * S + slot_iota
    score = jnp.where(active_flags, score, score + (1 << 17) * S)
    score = score.at[0, 0, S - 1].set(-1)
    order = jnp.argsort(score, axis=-1, stable=True).astype(jnp.int32)
    sends = order[:, :, :G]
    array_shape = (PX, PY, S, K)
    local = (jax.random.randint(keys[2], array_shape, 0, 1 << 20).astype(jnp.int32) % counts[:, :, None, None]).astype(jnp.int32)
    raw = jax.random.randint(keys[3], array_shape, 0, 8).astype(jnp.int32)
    direction = raw + (raw >= 4).astype(jnp.int32)
    row = lax.broadcasted_iota(jnp.int32, array_shape, 0) + direction // 3 - 1
    col = lax.broadcasted_iota(jnp.int32, array_shape, 1) + direction % 3 - 1
    valid = (row >= 0) & (row < PX) & (col >= 0) & (col < PY)
    entry = lax.broadcasted_iota(jnp.int32, array_shape, 3)
    ghost = valid & (entry >= 3) & (jax.random.randint(keys[4], array_shape, 0, 2) == 1)
    ghost_slot = jax.random.randint(keys[5], array_shape, 0, G).astype(jnp.int32)
    own_slot = lax.broadcasted_iota(jnp.int32, array_shape, 2)
    neighbour_directions = jnp.where(ghost, direction, 4)
    slot_table = jnp.where(ghost, ghost_slot, local)
    neighbour_directions = jnp.where(entry == 0, 4, neighbour_directions).astype(jnp.int32)
    slot_table = jnp.where(entry == 0, own_slot, slot_table).astype(jnp.int32)
    return (counts, sends, neighbour_directions, slot_table)


def draw_counts(key, part):
    return layout(key)[0]


def draw_send_list(key, part):
    return layout(key)[1]


def draw_nbr_dir(key, part):
    return layout(key)[2]


def draw_nbr_slot(key, part):
    return layout(key)[3]


def draw_particles(key, part):
    key = jax.random.fold_in(key, 11)
    first, second = jax.random.split(key, 2)
    place = jax.random.uniform(first, (PX, PY, S, 3, TILE), jnp.float32)
    motion = jnp.clip(jax.random.normal(second, (PX, PY, S, 3, TILE), jnp.float32), -5.0, 5.0)
    return jnp.concatenate([place, motion], axis=3)


def draw_dinv(key, part):
    key = jax.random.fold_in(key, 12)
    first, second = jax.random.split(key, 2)
    array_shape = (PX, PY, S, TILE, TILE)
    rows = lax.broadcasted_iota(jnp.int32, array_shape, 3)
    cols = lax.broadcasted_iota(jnp.int32, array_shape, 4)
    diag = jax.random.uniform(first, (PX, PY, S, TILE, 1), jnp.float32, 0.6, 1.4)
    noise = jnp.clip(jax.random.normal(second, array_shape, jnp.float32), -4.0, 4.0) * (0.3 / math.sqrt(TILE))
    return jnp.where(rows == cols, diag, 0.0) + noise


def setup_inputs(seed: int = 0) -> dict:
    streams_of = jax.random.split(jax.random.key(seed), 9)
    particles = draw_particles(jax.random.fold_in(streams_of[8], 71), 0)
    dinv = draw_dinv(jax.random.fold_in(streams_of[8], 71), 0)
    low_bound = jnp.clip(jax.random.uniform(streams_of[2], (1,), jnp.float32, 0.3, 0.6), 0.3, 0.6)
    high_bound = jnp.clip(jax.random.uniform(streams_of[3], (1,), jnp.float32, 2.2, 3.2), 2.2, 3.2)
    counts = draw_counts(jax.random.fold_in(streams_of[8], 71), 0)
    send_list = draw_send_list(jax.random.fold_in(streams_of[8], 71), 0)
    nbr_dir = draw_nbr_dir(jax.random.fold_in(streams_of[8], 71), 0)
    nbr_slot = draw_nbr_slot(jax.random.fold_in(streams_of[8], 71), 0)
    return dict(particles=particles, dinv=dinv, low_bound=low_bound, high_bound=high_bound, counts=counts, send_list=send_list, nbr_dir=nbr_dir, nbr_slot=nbr_slot)


tile_cluster = 4
radius_sq = 0.25
viscosity = 0.5
source_gain = 8.0
gradient_gain = 4.0


def pair_sums(owned_positions, pos_ext, particle_index, feat_ext):
    slot_count = owned_positions.shape[0]
    tile_width = owned_positions.shape[2]
    block_list = slot_count // tile_cluster

    def one_block(args):
        block_pos, block_index = args
        near_pos = pos_ext[block_index]
        near_feat = feat_ext[block_index]
        dist = jnp.zeros(block_index.shape + (tile_width, tile_width), jnp.float32)
        for comp in range(3):
            delta = block_pos[:, None, comp, :, None] - near_pos[:, :, comp, None, :]
            dist = dist + delta * delta
        inside = jnp.maximum(1.0 - dist / radius_sq, 0.0)
        kernel_weight = inside * inside * inside
        grand_total = jnp.sum(kernel_weight, axis=(1, 3))
        blended_values = jnp.einsum("bkac,bkfc->bfa", kernel_weight, near_feat, precision=lax.Precision.HIGHEST)
        return grand_total, blended_values

    grand_total, blended_values = lax.map(one_block, (owned_positions.reshape(block_list, tile_cluster, 3, tile_width), particle_index.reshape(block_list, tile_cluster, -1)))
    return grand_total.reshape(slot_count, tile_width), blended_values.reshape((slot_count,) + blended_values.shape[2:])


def ghost_pad(field, send_list):
    ghosts = jax.vmap(jax.vmap(lambda whole, picks: whole[picks]))(field, send_list)
    return jnp.pad(ghosts, ((1, 1), (1, 1), (0, 0), (0, 0), (0, 0)))


def cycle_of(padded, row, col):
    zero = jnp.zeros((), jnp.int32)
    block = lax.dynamic_slice(padded, (row, col, zero, zero, zero), (3, 3) + padded.shape[2:])
    return block.reshape((9 * padded.shape[2],) + padded.shape[3:])


def map_devices(func):
    flat = jnp.arange(PX * PY, dtype=jnp.int32)
    out = lax.map(lambda dev: func(dev // PY, dev % PY), flat)
    return out.reshape((PX, PY) + out.shape[1:])


def reference(particles, dinv, low_bound, high_bound, counts, send_list, nbr_dir, nbr_slot):
    index_all = jnp.where(nbr_dir == 4, nbr_slot, S + nbr_dir * G + nbr_slot).astype(jnp.int32)
    positions = particles[:, :, :, :3]
    part_pad = ghost_pad(particles, send_list)

    def ext_pos_of(row, col):
        return jnp.concatenate([positions[row, col], cycle_of(part_pad, row, col)[:, :3]], axis=0)

    def viscous(row, col):
        owned_particles = particles[row, col]
        ext = jnp.concatenate([owned_particles, cycle_of(part_pad, row, col)], axis=0)
        grand_total, blended_values = pair_sums(owned_particles[:, :3], ext[:, :3], index_all[row, col], ext[:, 3:])
        speed = owned_particles[:, 3:]
        return speed + viscosity * (blended_values / grand_total[:, None, :] - speed)

    ustar = map_devices(viscous)
    ustar_pad = ghost_pad(ustar, send_list)

    def source_of(row, col):
        ext_pos = ext_pos_of(row, col)
        ext_u = jnp.concatenate([ustar[row, col], cycle_of(ustar_pad, row, col)], axis=0)
        feat = jnp.concatenate([ext_u, ext_pos, jnp.sum(ext_pos * ext_u, axis=1, keepdims=True)], axis=1)
        place = positions[row, col]
        grand_total, blended_values = pair_sums(place, ext_pos, index_all[row, col], feat)
        flow = ustar[row, col]
        value = grand_total * jnp.sum(place * flow, axis=1) - jnp.sum(place * blended_values[:, 0:3], axis=1) - jnp.sum(flow * blended_values[:, 3:6], axis=1) + blended_values[:, 6]
        return source_gain * value / grand_total

    source = map_devices(source_of)

    def operator(field):
        field_pad = ghost_pad(field[:, :, :, None, :], send_list)

        def local_apply(row, col):
            ext_field = jnp.concatenate([field[row, col][:, None, :], cycle_of(field_pad, row, col)], axis=0)
            grand_total, blended_values = pair_sums(positions[row, col], ext_pos_of(row, col), index_all[row, col], ext_field)
            return 2.0 * field[row, col] - blended_values[:, 0] / grand_total

        return map_devices(local_apply)

    def precondition(resid):
        return jnp.einsum("xysab,xysb->xysa", dinv, resid, precision=lax.Precision.HIGHEST)

    theta = (high_bound[0] + low_bound[0]) / 2.0
    delta = (high_bound[0] - low_bound[0]) / 2.0
    sigma = theta / delta
    rho = 1.0 / sigma
    resid = source
    step_dir = precondition(resid) / theta
    press = jnp.zeros_like(source)
    for it in range(ITERS):
        press = press + step_dir
        if it + 1 < ITERS:
            resid = resid - operator(step_dir)
            rho_new = 1.0 / (2.0 * sigma - rho)
            step_dir = rho_new * rho * step_dir + (2.0 * rho_new / delta) * precondition(resid)
            rho = rho_new

    press_pad = ghost_pad(press[:, :, :, None, :], send_list)

    def gradient(row, col):
        ext_pos = ext_pos_of(row, col)
        ext_p = jnp.concatenate([press[row, col][:, None, :], cycle_of(press_pad, row, col)], axis=0)
        feat = jnp.concatenate([ext_p * ext_pos, ext_p, ext_pos], axis=1)
        place = positions[row, col]
        grand_total, blended_values = pair_sums(place, ext_pos, index_all[row, col], feat)
        own_p = press[row, col][:, None, :]
        value = blended_values[:, 0:3] - place * blended_values[:, 3:4] - own_p * blended_values[:, 4:7] + own_p * place * grand_total[:, None, :]
        return value / grand_total[:, None, :]

    grad = map_devices(gradient)
    active_flags = lax.broadcasted_iota(jnp.int32, (PX, PY, S), 2) < counts[:, :, None]
    pressure = jnp.where(active_flags[:, :, :, None], press, 0.0)
    velocity = jnp.where(active_flags[:, :, :, None, None], ustar - gradient_gain * grad, 0.0)
    return pressure, velocity
```

```python
import functools

import jax
import jax.numpy as jnp
from jax import lax
from jax.experimental import pallas as pl
from jax.experimental.pallas import tpu as pltpu
from jax.sharding import PartitionSpec as P

ITERS = 3
MESH = pl.DeviceIdType.MESH
CODES = (0, 1, 2, 3, 5, 6, 7, 8)
F32 = jnp.float32
BF16 = jnp.bfloat16


def split(value):
    head = value.astype(BF16).astype(F32)
    return jnp.concatenate([head, value - head], axis=0).astype(BF16)


def split_row(row):
    wide = jnp.broadcast_to(row, (8, row.shape[1]))
    head = wide.astype(BF16).astype(F32)
    first = lax.broadcasted_iota(jnp.int32, wide.shape, 0) == 0
    return jnp.where(first, head, wide - head).astype(BF16)


def kernel(px, py, sizes, part_ref, dinv_ref, low_ref, high_ref, counts_ref, send_ref, dir_ref, slot_ref,
           press_ref, vel_ref,
           w, draw, dinv_t, pos, mot, flow, flow_own, step0, step1, step2, step_own, total_p, sums, src, ztot, mres,
           st_pos, st_mot, st_flow, st_step0, st_step1, st_step2, dsem, send_sem, recv_sem):
    S, G, K, T = sizes
    steps = (step0, step1, step2)
    st_step = (st_step0, st_step1, st_step2)
    i = lax.axis_index("gx")
    j = lax.axis_index("gy")

    def inside(di, dj):
        return (i + di >= 0) & (i + di < px) & (j + dj >= 0) & (j + dj < py)

    barrier = pltpu.get_barrier_semaphore()
    straight = ((-1, 0), (1, 0), (0, -1), (0, 1))
    for di, dj in straight:
        @pl.when(inside(di, dj))
        def _():
            pl.semaphore_signal(barrier, inc=1, device_id=(i + di, j + dj), device_id_type=MESH)

    load_dinv = pltpu.make_async_copy(dinv_ref.at[0, 0], draw, dsem)
    load_dinv.start()

    def make_tile(s):
        block = part_ref[0, 0, s]
        place = 2.0 * block[0:3] - 1.0
        square = place * place
        norm = -(square[0:1] + square[1:2] + square[2:3])
        return (jnp.concatenate([place, norm], axis=0),
                jnp.concatenate([block[3:6], jnp.ones((1, T), F32)], axis=0))

    def stage_tile(g, _):
        st_pos[g], st_mot[g] = make_tile(send_ref[0, 0, g])
        return 0

    lax.fori_loop(0, G, stage_tile, 0, unroll=4)
    pl.semaphore_wait(barrier, sum(inside(di, dj).astype(jnp.int32) for di, dj in straight))

    def ghosts(ext, code):
        return ext.at[pl.ds(S + code * G, G)]

    def transfer(e, ext, source, code):
        di, dj = code // 3 - 1, code % 3 - 1
        if di != 0 and dj != 0:
            source = ghosts(ext, 3 * (di + 1) + 1)
            target = (i, j - dj)
        else:
            target = (i - di, j - dj)
        return pltpu.make_async_remote_copy(
            src_ref=source, dst_ref=ghosts(ext, code), send_sem=send_sem.at[e, code],
            recv_sem=recv_sem.at[e, code], device_id=target, device_id_type=MESH)

    def sends(code):
        di, dj = code // 3 - 1, code % 3 - 1
        if di != 0 and dj != 0:
            return inside(di, 0) & inside(0, -dj)
        return inside(-di, -dj)

    def begin(e, ext, staged):
        for code in (1, 7, 3, 5):
            @pl.when(sends(code))
            def _():
                transfer(e, ext, staged, code).start()

    def forward(e, ext, staged):
        for code in (1, 7):
            @pl.when(inside(code // 3 - 1, 0))
            def _():
                transfer(e, ext, staged, code).wait_recv()
            for follow in (code - 1, code + 1):
                @pl.when(sends(follow))
                def _():
                    transfer(e, ext, staged, follow).start()

    def arrive(e, ext, staged):
        for code in (3, 5, 0, 2, 6, 8):
            @pl.when(inside(code // 3 - 1, code % 3 - 1))
            def _():
                transfer(e, ext, staged, code).wait_recv()

    def finish(e, ext, staged):
        for code in CODES:
            @pl.when(sends(code))
            def _():
                transfer(e, ext, staged, code).wait_send()

    begin(0, pos, st_pos)
    begin(1, mot, st_mot)

    def own_tile(s, _):
        pos[s], mot[s] = make_tile(s)
        return 0

    lax.fori_loop(0, S, own_tile, 0, unroll=4)
    load_dinv.wait()
    forward(0, pos, st_pos)
    forward(1, mot, st_mot)

    def turn(s, _):
        dinv_t[s] = split(draw[s].T)
        return 0

    lax.fori_loop(0, S, turn, 0, unroll=2)
    arrive(0, pos, st_pos)

    def neighbour(s, k):
        code = dir_ref[0, 0, s, k]
        slot = slot_ref[0, 0, s, k]
        return jnp.where(code == 4, slot, S + code * G + slot)

    row4 = lax.broadcasted_iota(jnp.int32, (4, T), 0)
    unit4 = jnp.where(row4 == 0, 1.0, 0.0)

    def weigh(s, _):
        own = pos[s]
        own_rows = jnp.concatenate([jnp.where(row4 == 3, 1.0, 2.0 * own), jnp.where(row4 == 0, 1.0 + own[3:4], 0.0)], axis=0)
        head = own_rows.astype(BF16).astype(F32)
        rest = own_rows - head
        own_side = jnp.concatenate([head, head, rest, rest], axis=0).astype(BF16)
        for k in range(K):
            near = split(jnp.concatenate([pos[neighbour(s, k)], unit4], axis=0))
            near_side = jnp.concatenate([near, near], axis=0)
            value = lax.dot_general(near_side, own_side, (((0,), (0,)), ((), ())), preferred_element_type=F32)
            value = jnp.maximum(value, 0.0)
            value = value * value * value
            top = value.astype(BF16)
            w[s, 2 * k * T:(2 * k + 1) * T, :] = top
            w[s, (2 * k + 1) * T:(2 * k + 2) * T, :] = (value - top.astype(F32)).astype(BF16)
        return 0

    lax.fori_loop(0, S, weigh, 0, unroll=2)
    arrive(1, mot, st_mot)

    def apply(s, feature):
        parts = []
        for k in range(K):
            part = feature(neighbour(s, k))
            parts += [part, part]
        return jnp.dot(jnp.concatenate(parts, axis=1), w[s], preferred_element_type=F32)

    def viscous(s, _):
        out = apply(s, lambda n: split(jnp.concatenate([pos[n], mot[n]], axis=0)))
        out = out[0:8] + out[8:16]
        sums[s] = out
        speed = mot[s]
        ustar = speed + 0.5 * (out[4:8] / out[7:8] - speed)
        both = pos[s] * ustar
        rows = jnp.concatenate([ustar[0:3], both[0:1] + both[1:2] + both[2:3]], axis=0)
        flow[s] = rows
        flow_own[s] = rows
        return 0

    lax.fori_loop(0, S, viscous, 0, unroll=4)

    def stage_flow(g, _):
        st_flow[g] = flow_own[send_ref[0, 0, g]]
        return 0

    def exchange(e, ext, staged):
        begin(e, ext, staged)
        forward(e, ext, staged)
        arrive(e, ext, staged)

    lax.fori_loop(0, G, stage_flow, 0, unroll=8)
    exchange(2, flow, st_flow)

    def source(s, _):
        out = apply(s, lambda n: split(flow[n]))
        out = out[0:4] + out[4:8]
        known = sums[s]
        place = pos[s]
        own = flow[s]
        total = known[7:8]
        cross = place * out + own * known[0:4]
        value = total * own[3:4] - (cross[0:1] + cross[1:2] + cross[2:3]) + out[3:4]
        src[pl.ds(s, 1), :] = 4.0 * value / total
        ztot[pl.ds(s, 1), :] = total
        return 0

    lax.fori_loop(0, S, source, 0, unroll=4)

    def precondition():
        def one(s, _):
            row = split_row(src[pl.ds(s, 1), :])
            out = jnp.dot(jnp.concatenate([row, row], axis=1), dinv_t[s], preferred_element_type=F32)
            mres[pl.ds(s, 1), :] = out[0:1] + out[1:2]
            return 0

        lax.fori_loop(0, S, one, 0, unroll=8)
        return mres[...]

    low = jnp.full((1, T), low_ref[0], F32)
    high = jnp.full((1, T), high_ref[0], F32)
    theta = (high + low) / 2.0
    delta = (high - low) / 2.0
    sigma = theta / delta
    rho = 1.0 / sigma
    step = precondition() / theta
    for it in range(ITERS):
        ext = steps[it]
        staged = st_step[it]
        ext[0:S] = step
        step_own[...] = step

        def stage_step(g, _):
            staged[pl.ds(g, 1), :] = step_own[pl.ds(send_ref[0, 0, g], 1), :]
            return 0

        lax.fori_loop(0, G, stage_step, 0, unroll=8)
        exchange(3 + it, ext, staged)
        if it + 1 < ITERS:
            def operate(s, _):
                out = apply(s, lambda n: split_row(ext[pl.ds(n, 1), :]))
                mres[pl.ds(s, 1), :] = out[0:1] + out[1:2]
                return 0

            lax.fori_loop(0, S, operate, 0, unroll=4)
            src[...] = src[...] - (2.0 * step - mres[...] / ztot[...])
            rho_new = 1.0 / (2.0 * sigma - rho)
            step = rho_new * rho * step + 2.0 * rho_new / delta * precondition()
            rho = rho_new

    total_p[...] = step0[...] + step1[...] + step2[...]
    count = counts_ref[0, 0]
    live = lax.broadcasted_iota(jnp.int32, (S, T), 0) < count
    press_ref[0, 0] = jnp.where(live, total_p[0:S], 0.0)

    def gradient(s, _):
        def feature(n):
            return split(jnp.where(row4 == 3, 1.0, pos[n]) * total_p[pl.ds(n, 1), :])

        out = apply(s, feature)
        out = out[0:4] + out[4:8]
        known = sums[s]
        place = pos[s]
        own_p = total_p[pl.ds(s, 1), :]
        total = known[7:8]
        value = out - place * out[3:4] - own_p * known[0:4] + own_p * place * total
        result = flow[s] - 2.0 * (value / total)
        alive = jnp.full((3, T), count, jnp.int32) > s
        vel_ref[0, 0, s] = jnp.where(alive, result[0:3], 0.0)
        return 0

    lax.fori_loop(0, S, gradient, 0, unroll=4)

    finish(0, pos, st_pos)
    finish(1, mot, st_mot)
    finish(2, flow, st_flow)
    for it in range(ITERS):
        finish(3 + it, steps[it], st_step[it])


def body(px, py, particles, dinv, low_bound, high_bound, counts, send_list, nbr_dir, nbr_slot):
    S, T = particles.shape[2], particles.shape[4]
    G = send_list.shape[2]
    K = nbr_dir.shape[3]
    N = S + 9 * G
    vmem = pl.BlockSpec(memory_space=pltpu.VMEM)
    smem = pl.BlockSpec(memory_space=pltpu.SMEM)
    exchanges = 3 + ITERS
    return pl.pallas_call(
        functools.partial(kernel, px, py, (S, G, K, T)),
        out_shape=(jax.ShapeDtypeStruct((1, 1, S, T), F32), jax.ShapeDtypeStruct((1, 1, S, 3, T), F32)),
        in_specs=[vmem, pl.BlockSpec(memory_space=pl.ANY), smem, smem, smem, smem, smem, smem],
        out_specs=(vmem, vmem),
        scratch_shapes=[
            pltpu.VMEM((S, 2 * K * T, T), BF16),
            pltpu.VMEM((S, T, T), F32),
            pltpu.VMEM((S, 2 * T, T), BF16),
            pltpu.VMEM((N, 4, T), F32),
            pltpu.VMEM((N, 4, T), F32),
            pltpu.VMEM((N, 4, T), F32),
            pltpu.VMEM((S, 4, T), F32),
            *[pltpu.VMEM((N, T), F32)] * ITERS,
            pltpu.VMEM((S, T), F32),
            pltpu.VMEM((N, T), F32),
            pltpu.VMEM((S, 8, T), F32),
            pltpu.VMEM((S, T), F32),
            pltpu.VMEM((S, T), F32),
            pltpu.VMEM((S, T), F32),
            pltpu.VMEM((G, 4, T), F32),
            pltpu.VMEM((G, 4, T), F32),
            pltpu.VMEM((G, 4, T), F32),
            *[pltpu.VMEM((G, T), F32)] * ITERS,
            pltpu.SemaphoreType.DMA,
            pltpu.SemaphoreType.DMA((exchanges, 9)),
            pltpu.SemaphoreType.DMA((exchanges, 9)),
        ],
        compiler_params=pltpu.CompilerParams(
            collective_id=0, has_side_effects=True, vmem_limit_bytes=48 << 20),
    )(particles, dinv, low_bound, high_bound, counts, send_list, nbr_dir, nbr_slot)


def solution(mesh):
    placed = (
        P("gx", "gy", None, None, None),
        P("gx", "gy", None, None, None),
        P(),
        P(),
        P("gx", "gy"),
        P("gx", "gy", None),
        P("gx", "gy", None, None),
        P("gx", "gy", None, None),
    )
    return jax.shard_map(
        functools.partial(body, mesh.shape["gx"], mesh.shape["gy"]),
        mesh=mesh,
        in_specs=placed,
        out_specs=(P("gx", "gy", None, None), P("gx", "gy", None, None, None)),
        check_vma=False,
    )
```

```python
import functools

import jax
import jax.numpy as jnp
from jax import lax
from jax.experimental import pallas as pl
from jax.experimental.pallas import tpu as pltpu
from jax.sharding import PartitionSpec as P

ITERS = 3
MESH = pl.DeviceIdType.MESH
DIRECT = (3, 4, 5)
CODES = (0, 1, 2, 3, 5, 6, 7, 8)
F32 = jnp.float32
BF16 = jnp.bfloat16


def split(value):
    head = value.astype(BF16).astype(F32)
    return jnp.concatenate([head, value - head], axis=0).astype(BF16)


def split_row(row):
    wide = jnp.broadcast_to(row, (8, row.shape[1]))
    head = wide.astype(BF16).astype(F32)
    first = lax.broadcasted_iota(jnp.int32, wide.shape, 0) == 0
    return jnp.where(first, head, wide - head).astype(BF16)


def kernel(px, py, sizes, part_ref, dinv_ref, low_ref, high_ref, counts_ref, send_ref, dir_ref, slot_ref,
           press_ref, vel_ref,
           w, draw, dinv_t, pos, mot, flow, flow_own, step0, step1, step2, step_own, total_p, sums, src, ztot, mres,
           st_pos, st_mot, st_flow, st_step0, st_step1, st_step2, dsem, send_sem, recv_sem):
    S, G, K, T = sizes
    steps = (step0, step1, step2)
    st_step = (st_step0, st_step1, st_step2)
    i = lax.axis_index("gx")
    j = lax.axis_index("gy")

    def inside(di, dj):
        return (i + di >= 0) & (i + di < px) & (j + dj >= 0) & (j + dj < py)

    barrier = pltpu.get_barrier_semaphore()
    straight = tuple((c // 3 - 1, c % 3 - 1) for c in CODES)
    for di, dj in straight:
        @pl.when(inside(di, dj))
        def _():
            pl.semaphore_signal(barrier, inc=1, device_id=(i + di, j + dj), device_id_type=MESH)

    load_dinv = pltpu.make_async_copy(dinv_ref.at[0, 0], draw, dsem)
    load_dinv.start()

    def make_tile(s):
        rows = [part_ref[0, 0, c, pl.ds(s, 1), :] for c in range(6)]
        place = [2.0 * row - 1.0 for row in rows[:3]]
        norm = -(place[0] * place[0] + place[1] * place[1] + place[2] * place[2])
        return (jnp.concatenate(place + [norm], axis=0),
                jnp.concatenate(rows[3:] + [jnp.ones((1, T), F32)], axis=0))

    def stage_tile(g, _):
        st_pos[g], st_mot[g] = make_tile(send_ref[0, 0, g])
        return 0

    lax.fori_loop(0, G, stage_tile, 0, unroll=4)
    pl.semaphore_wait(barrier, sum(inside(di, dj).astype(jnp.int32) for di, dj in straight))

    def ghosts(ext, code):
        return ext.at[pl.ds(S + code * G, G)]

    def transfer(e, ext, source, code):
        di, dj = code // 3 - 1, code % 3 - 1
        if di != 0 and dj != 0 and e not in DIRECT:
            source = ghosts(ext, 3 * (di + 1) + 1)
            target = (i, j - dj)
        else:
            target = (i - di, j - dj)
        return pltpu.make_async_remote_copy(
            src_ref=source, dst_ref=ghosts(ext, code), send_sem=send_sem.at[e, code],
            recv_sem=recv_sem.at[e, code], device_id=target, device_id_type=MESH)

    def sends(e, code):
        di, dj = code // 3 - 1, code % 3 - 1
        if di != 0 and dj != 0 and e not in DIRECT:
            return inside(di, 0) & inside(0, -dj)
        return inside(-di, -dj)

    def begin(e, ext, staged):
        for code in (0, 2, 6, 8, 1, 7, 3, 5) if e in DIRECT else (1, 7, 3, 5):
            @pl.when(sends(e, code))
            def _():
                transfer(e, ext, staged, code).start()

    def forward(e, ext, staged):
        if e in DIRECT:
            return
        for code in (1, 7):
            @pl.when(inside(code // 3 - 1, 0))
            def _():
                transfer(e, ext, staged, code).wait_recv()
            for follow in (code - 1, code + 1):
                @pl.when(sends(e, follow))
                def _():
                    transfer(e, ext, staged, follow).start()

    def arrive(e, ext, staged):
        for code in CODES if e in DIRECT else (3, 5, 0, 2, 6, 8):
            @pl.when(inside(code // 3 - 1, code % 3 - 1))
            def _():
                transfer(e, ext, staged, code).wait_recv()

    def finish(e, ext, staged):
        for code in CODES:
            @pl.when(sends(e, code))
            def _():
                transfer(e, ext, staged, code).wait_send()

    begin(0, pos, st_pos)
    begin(1, mot, st_mot)

    def own_tile(s, _):
        pos[s], mot[s] = make_tile(s)
        return 0

    lax.fori_loop(0, S, own_tile, 0, unroll=4)
    forward(0, pos, st_pos)
    load_dinv.wait()

    def turn(s, _):
        dinv_t[s] = split(draw[s].T)
        return 0

    lax.fori_loop(0, S, turn, 0, unroll=2)
    forward(1, mot, st_mot)
    arrive(0, pos, st_pos)

    def neighbour(s, k):
        code = dir_ref[0, 0, k, s]
        slot = slot_ref[0, 0, k, s]
        return jnp.where(code == 4, slot, S + code * G + slot)

    row4 = lax.broadcasted_iota(jnp.int32, (4, T), 0)
    unit4 = jnp.where(row4 == 0, 1.0, 0.0)

    def weigh(s, _):
        own = pos[s]
        own_rows = jnp.concatenate([jnp.where(row4 == 3, 1.0, 2.0 * own), jnp.where(row4 == 0, 1.0 + own[3:4], 0.0)], axis=0)
        head = own_rows.astype(BF16).astype(F32)
        rest = own_rows - head
        own_side = jnp.concatenate([head, head, rest, rest], axis=0).astype(BF16)
        for k in range(K):
            near = split(jnp.concatenate([pos[neighbour(s, k)], unit4], axis=0))
            near_side = jnp.concatenate([near, near], axis=0)
            value = lax.dot_general(near_side, own_side, (((0,), (0,)), ((), ())), preferred_element_type=F32)
            value = jnp.maximum(value, 0.0)
            value = value * value * value
            top = value.astype(BF16)
            w[s, 2 * k * T:(2 * k + 1) * T, :] = top
            w[s, (2 * k + 1) * T:(2 * k + 2) * T, :] = (value - top.astype(F32)).astype(BF16)
        return 0

    lax.fori_loop(0, S, weigh, 0, unroll=4)
    arrive(1, mot, st_mot)

    def apply(s, feature):
        parts = []
        for k in range(K):
            part = feature(neighbour(s, k))
            parts += [part, part]
        return jnp.dot(jnp.concatenate(parts, axis=1), w[s], preferred_element_type=F32)

    def viscous(s, _):
        out = apply(s, lambda n: split(jnp.concatenate([pos[n], mot[n]], axis=0)))
        out = out[0:8] + out[8:16]
        sums[s] = out
        speed = mot[s]
        ustar = speed + 0.5 * (out[4:8] / out[7:8] - speed)
        both = pos[s] * ustar
        rows = jnp.concatenate([ustar[0:3], both[0:1] + both[1:2] + both[2:3]], axis=0)
        flow[s] = rows
        flow_own[s] = rows
        return 0

    lax.fori_loop(0, S, viscous, 0, unroll=4)

    def stage_flow(g, _):
        st_flow[g] = flow_own[send_ref[0, 0, g]]
        return 0

    def exchange(e, ext, staged):
        begin(e, ext, staged)
        forward(e, ext, staged)
        arrive(e, ext, staged)

    lax.fori_loop(0, G, stage_flow, 0, unroll=8)
    exchange(2, flow, st_flow)

    def source(s, _):
        out = apply(s, lambda n: split(flow[n]))
        out = out[0:4] + out[4:8]
        known = sums[s]
        place = pos[s]
        own = flow[s]
        total = known[7:8]
        cross = place * out + own * known[0:4]
        value = total * own[3:4] - (cross[0:1] + cross[1:2] + cross[2:3]) + out[3:4]
        src[pl.ds(s, 1), :] = 4.0 * value / total
        ztot[pl.ds(s, 1), :] = total
        return 0

    lax.fori_loop(0, S, source, 0, unroll=4)

    def precondition():
        def one(s, _):
            row = split_row(src[pl.ds(s, 1), :])
            out = jnp.dot(jnp.concatenate([row, row], axis=1), dinv_t[s], preferred_element_type=F32)
            mres[pl.ds(s, 1), :] = out[0:1] + out[1:2]
            return 0

        lax.fori_loop(0, S, one, 0, unroll=8)
        return mres[...]

    low = jnp.full((1, T), low_ref[0], F32)
    high = jnp.full((1, T), high_ref[0], F32)
    theta = (high + low) / 2.0
    delta = (high - low) / 2.0
    sigma = theta / delta
    rho = 1.0 / sigma
    step = precondition() / theta
    for it in range(ITERS):
        ext = steps[it]
        staged = st_step[it]
        ext[0:S] = step
        step_own[...] = step

        def stage_step(g, _):
            staged[pl.ds(g, 1), :] = step_own[pl.ds(send_ref[0, 0, g], 1), :]
            return 0

        lax.fori_loop(0, G, stage_step, 0, unroll=8)
        exchange(3 + it, ext, staged)
        if it + 1 < ITERS:
            def operate(s, _):
                out = apply(s, lambda n: split_row(ext[pl.ds(n, 1), :]))
                mres[pl.ds(s, 1), :] = out[0:1] + out[1:2]
                return 0

            lax.fori_loop(0, S, operate, 0, unroll=4)
            src[...] = src[...] - (2.0 * step - mres[...] / ztot[...])
            rho_new = 1.0 / (2.0 * sigma - rho)
            step = rho_new * rho * step + 2.0 * rho_new / delta * precondition()
            rho = rho_new

    total_p[...] = step0[...] + step1[...] + step2[...]
    count = counts_ref[0, 0]
    live = lax.broadcasted_iota(jnp.int32, (S, T), 0) < count
    press_ref[0, 0] = jnp.where(live, total_p[0:S], 0.0)

    def gradient(s, _):
        def feature(n):
            return split(jnp.where(row4 == 3, 1.0, pos[n]) * total_p[pl.ds(n, 1), :])

        out = apply(s, feature)
        out = out[0:4] + out[4:8]
        known = sums[s]
        place = pos[s]
        own_p = total_p[pl.ds(s, 1), :]
        total = known[7:8]
        value = out - place * out[3:4] - own_p * known[0:4] + own_p * place * total
        result = flow[s] - 2.0 * (value / total)
        alive = jnp.full((3, T), count, jnp.int32) > s
        result = jnp.where(alive, result[0:3], 0.0)
        for c in range(3):
            vel_ref[0, 0, c, pl.ds(s, 1), :] = result[c:c + 1]
        return 0

    lax.fori_loop(0, S, gradient, 0, unroll=4)

    finish(0, pos, st_pos)
    finish(1, mot, st_mot)
    finish(2, flow, st_flow)
    for it in range(ITERS):
        finish(3 + it, steps[it], st_step[it])


def body(px, py, particles, dinv, low_bound, high_bound, counts, send_list, nbr_dir, nbr_slot):
    S, T = particles.shape[2], particles.shape[4]
    G = send_list.shape[2]
    K = nbr_dir.shape[3]
    N = S + 9 * G
    vmem = pl.BlockSpec(memory_space=pltpu.VMEM)
    smem = pl.BlockSpec(memory_space=pltpu.SMEM)
    exchanges = 3 + ITERS
    swap = lambda array: jnp.swapaxes(array, 2, 3)
    press, vel = pl.pallas_call(
        functools.partial(kernel, px, py, (S, G, K, T)),
        out_shape=(jax.ShapeDtypeStruct((1, 1, S, T), F32), jax.ShapeDtypeStruct((1, 1, 3, S, T), F32)),
        in_specs=[vmem, pl.BlockSpec(memory_space=pltpu.HBM), smem, smem, smem, smem, smem, smem],
        out_specs=(vmem, vmem),
        scratch_shapes=[
            pltpu.VMEM((S, 2 * K * T, T), BF16),
            pltpu.VMEM((S, T, T), F32),
            pltpu.VMEM((S, 2 * T, T), BF16),
            pltpu.VMEM((N, 4, T), F32),
            pltpu.VMEM((N, 4, T), F32),
            pltpu.VMEM((N, 4, T), F32),
            pltpu.VMEM((S, 4, T), F32),
            *[pltpu.VMEM((N, T), F32)] * ITERS,
            pltpu.VMEM((S, T), F32),
            pltpu.VMEM((N, T), F32),
            pltpu.VMEM((S, 8, T), F32),
            pltpu.VMEM((S, T), F32),
            pltpu.VMEM((S, T), F32),
            pltpu.VMEM((S, T), F32),
            pltpu.VMEM((G, 4, T), F32),
            pltpu.VMEM((G, 4, T), F32),
            pltpu.VMEM((G, 4, T), F32),
            *[pltpu.VMEM((G, T), F32)] * ITERS,
            pltpu.SemaphoreType.DMA,
            pltpu.SemaphoreType.DMA((exchanges, 9)),
            pltpu.SemaphoreType.DMA((exchanges, 9)),
        ],
        compiler_params=pltpu.CompilerParams(
            collective_id=0, has_side_effects=True, vmem_limit_bytes=48 << 20),
    )(swap(particles), dinv, low_bound, high_bound, counts, send_list, swap(nbr_dir), swap(nbr_slot))
    return press, swap(vel)


def solution(mesh):
    placed = (
        P("gx", "gy", None, None, None),
        P("gx", "gy", None, None, None),
        P(),
        P(),
        P("gx", "gy"),
        P("gx", "gy", None),
        P("gx", "gy", None, None),
        P("gx", "gy", None, None),
    )
    return jax.shard_map(
        functools.partial(body, mesh.shape["gx"], mesh.shape["gy"]),
        mesh=mesh,
        in_specs=placed,
        out_specs=(P("gx", "gy", None, None), P("gx", "gy", None, None, None)),
        check_vma=False,
    )
```

```python
import functools

import jax
import jax.numpy as jnp
from jax import lax
from jax.experimental import pallas as pl
from jax.experimental.pallas import tpu as pltpu
from jax.sharding import PartitionSpec as P

ITERS = 3
MESH = pl.DeviceIdType.MESH
DIRECT = (3, 4, 5)
LATE = 6
CODES = (0, 1, 2, 3, 5, 6, 7, 8)
F32 = jnp.float32
BF16 = jnp.bfloat16


def split(value):
    head = value.astype(BF16).astype(F32)
    return jnp.concatenate([head, value - head], axis=0).astype(BF16)


def split_row(row):
    wide = jnp.broadcast_to(row, (8, row.shape[1]))
    head = wide.astype(BF16).astype(F32)
    first = lax.broadcasted_iota(jnp.int32, wide.shape, 0) == 0
    return jnp.where(first, head, wide - head).astype(BF16)


def kernel(px, py, sizes, part_ref, dinv_ref, low_ref, high_ref, counts_ref, send_ref, dir_ref, slot_ref,
           press_ref, vel_ref,
           w, draw, dinv_t, pos, mot, flow, step0, step1, step2, step_own, total_p, sums, src, ztot, mres,
           st_pos, st_mot, st_flow, st_late, st_step0, st_step1, st_step2, dsem, send_sem, recv_sem):
    S, G, K, T = sizes
    steps = (step0, step1, step2)
    st_step = (st_step0, st_step1, st_step2)
    i = lax.axis_index("gx")
    j = lax.axis_index("gy")

    def inside(di, dj):
        return (i + di >= 0) & (i + di < px) & (j + dj >= 0) & (j + dj < py)

    barrier = pltpu.get_barrier_semaphore()
    straight = tuple((c // 3 - 1, c % 3 - 1) for c in CODES)
    for di, dj in straight:
        @pl.when(inside(di, dj))
        def _():
            pl.semaphore_signal(barrier, inc=1, device_id=(i + di, j + dj), device_id_type=MESH)

    load_dinv = pltpu.make_async_copy(dinv_ref.at[0, 0], draw, dsem)
    load_dinv.start()

    def make_tile(s):
        rows = [part_ref[0, 0, c, pl.ds(s, 1), :] for c in range(6)]
        place = [2.0 * row - 1.0 for row in rows[:3]]
        norm = -(place[0] * place[0] + place[1] * place[1] + place[2] * place[2])
        return (jnp.concatenate(place + [norm], axis=0),
                jnp.concatenate(rows[3:] + [jnp.ones((1, T), F32)], axis=0))

    def stage_tile(g, _):
        st_pos[g], st_mot[g] = make_tile(send_ref[0, 0, g])
        return 0

    lax.fori_loop(0, G, stage_tile, 0, unroll=4)
    pl.semaphore_wait(barrier, sum(inside(di, dj).astype(jnp.int32) for di, dj in straight))

    half = G // 2

    def ghosts(e, ext, code):
        if e == 2:
            return ext.at[pl.ds(S + code * G, half)]
        if e == LATE:
            return ext.at[pl.ds(S + code * G + half, G - half)]
        return ext.at[pl.ds(S + code * G, G)]

    def transfer(e, ext, source, code):
        di, dj = code // 3 - 1, code % 3 - 1
        if di != 0 and dj != 0 and e not in DIRECT:
            source = ghosts(e, ext, 3 * (di + 1) + 1)
            target = (i, j - dj)
        else:
            target = (i - di, j - dj)
        return pltpu.make_async_remote_copy(
            src_ref=source, dst_ref=ghosts(e, ext, code), send_sem=send_sem.at[e, code],
            recv_sem=recv_sem.at[e, code], device_id=target, device_id_type=MESH)

    def sends(e, code):
        di, dj = code // 3 - 1, code % 3 - 1
        if di != 0 and dj != 0 and e not in DIRECT:
            return inside(di, 0) & inside(0, -dj)
        return inside(-di, -dj)

    def begin(e, ext, staged):
        for code in (0, 2, 6, 8, 1, 7, 3, 5) if e in DIRECT else (1, 7, 3, 5):
            @pl.when(sends(e, code))
            def _():
                transfer(e, ext, staged, code).start()

    def forward(e, ext, staged):
        if e in DIRECT:
            return
        for code in (1, 7):
            @pl.when(inside(code // 3 - 1, 0))
            def _():
                transfer(e, ext, staged, code).wait_recv()
            for follow in (code - 1, code + 1):
                @pl.when(sends(e, follow))
                def _():
                    transfer(e, ext, staged, follow).start()

    def arrive(e, ext, staged):
        for code in CODES if e in DIRECT else (3, 5, 0, 2, 6, 8):
            @pl.when(inside(code // 3 - 1, code % 3 - 1))
            def _():
                transfer(e, ext, staged, code).wait_recv()

    def finish(e, ext, staged):
        for code in CODES:
            @pl.when(sends(e, code))
            def _():
                transfer(e, ext, staged, code).wait_send()

    begin(0, pos, st_pos)
    begin(1, mot, st_mot)

    def own_tile(s, _):
        pos[s], mot[s] = make_tile(s)
        return 0

    lax.fori_loop(0, S, own_tile, 0, unroll=4)
    forward(0, pos, st_pos)
    load_dinv.wait()

    def turn(s, _):
        dinv_t[s] = split(draw[s].T)
        return 0

    lax.fori_loop(0, S, turn, 0, unroll=2)
    forward(1, mot, st_mot)
    arrive(0, pos, st_pos)

    def neighbour(s, k):
        code = dir_ref[0, 0, k, s]
        slot = slot_ref[0, 0, k, s]
        return jnp.where(code == 4, slot, S + code * G + slot)

    row4 = lax.broadcasted_iota(jnp.int32, (4, T), 0)
    unit4 = jnp.where(row4 == 0, 1.0, 0.0)

    def weigh(s, _):
        own = pos[s]
        own_rows = jnp.concatenate([jnp.where(row4 == 3, 1.0, 2.0 * own), jnp.where(row4 == 0, 1.0 + own[3:4], 0.0)], axis=0)
        head = own_rows.astype(BF16).astype(F32)
        rest = own_rows - head
        own_side = jnp.concatenate([head, head, rest, rest], axis=0).astype(BF16)
        for k in range(K):
            near = split(jnp.concatenate([pos[neighbour(s, k)], unit4], axis=0))
            near_side = jnp.concatenate([near, near], axis=0)
            value = lax.dot_general(near_side, own_side, (((0,), (0,)), ((), ())), preferred_element_type=F32)
            value = jnp.maximum(value, 0.0)
            value = value * value * value
            top = value.astype(BF16)
            w[s, 2 * k * T:(2 * k + 1) * T, :] = top
            w[s, (2 * k + 1) * T:(2 * k + 2) * T, :] = (value - top.astype(F32)).astype(BF16)
        return 0

    lax.fori_loop(0, S, weigh, 0, unroll=4)
    arrive(1, mot, st_mot)

    def apply(s, feature):
        parts = []
        for k in range(K):
            part = feature(neighbour(s, k))
            parts += [part, part]
        return jnp.dot(jnp.concatenate(parts, axis=1), w[s], preferred_element_type=F32)

    def ustar_of(s):
        out = apply(s, lambda n: split(jnp.concatenate([pos[n], mot[n]], axis=0)))
        out = out[0:8] + out[8:16]
        speed = mot[s]
        ustar = speed + 0.5 * (out[4:8] / out[7:8] - speed)
        both = pos[s] * ustar
        rows = jnp.concatenate([ustar[0:3], both[0:1] + both[1:2] + both[2:3]], axis=0)
        return out, rows

    def viscous(s, _):
        sums[s], flow[s] = ustar_of(s)
        return 0

    def lend_early(g, _):
        st_flow[g] = ustar_of(send_ref[0, 0, g])[1]
        return 0

    def lend_late(g, _):
        st_late[g - half] = ustar_of(send_ref[0, 0, g])[1]
        return 0

    def exchange(e, ext, staged):
        begin(e, ext, staged)
        forward(e, ext, staged)
        arrive(e, ext, staged)

    lax.fori_loop(0, half, lend_early, 0, unroll=4)
    begin(2, flow, st_flow)
    lax.fori_loop(half, G, lend_late, 0, unroll=4)
    begin(LATE, flow, st_late)
    forward(2, flow, st_flow)
    lax.fori_loop(0, S // 2, viscous, 0, unroll=8)
    forward(LATE, flow, st_late)
    lax.fori_loop(S // 2, S, viscous, 0, unroll=8)
    arrive(2, flow, st_flow)
    arrive(LATE, flow, st_late)

    def source(s, _):
        out = apply(s, lambda n: split(flow[n]))
        out = out[0:4] + out[4:8]
        known = sums[s]
        place = pos[s]
        own = flow[s]
        total = known[7:8]
        cross = place * out + own * known[0:4]
        value = total * own[3:4] - (cross[0:1] + cross[1:2] + cross[2:3]) + out[3:4]
        src[pl.ds(s, 1), :] = 4.0 * value / total
        ztot[pl.ds(s, 1), :] = total
        return 0

    lax.fori_loop(0, S, source, 0, unroll=8)

    def precondition():
        def one(s, _):
            row = split_row(src[pl.ds(s, 1), :])
            out = jnp.dot(jnp.concatenate([row, row], axis=1), dinv_t[s], preferred_element_type=F32)
            mres[pl.ds(s, 1), :] = out[0:1] + out[1:2]
            return 0

        lax.fori_loop(0, S, one, 0, unroll=8)
        return mres[...]

    low = jnp.full((1, T), low_ref[0], F32)
    high = jnp.full((1, T), high_ref[0], F32)
    theta = (high + low) / 2.0
    delta = (high - low) / 2.0
    sigma = theta / delta
    rho = 1.0 / sigma
    step = precondition() / theta
    for it in range(ITERS):
        ext = steps[it]
        staged = st_step[it]
        ext[0:S] = step
        step_own[...] = step

        def stage_step(g, _):
            staged[pl.ds(g, 1), :] = step_own[pl.ds(send_ref[0, 0, g], 1), :]
            return 0

        lax.fori_loop(0, G, stage_step, 0, unroll=8)
        exchange(3 + it, ext, staged)
        if it + 1 < ITERS:
            def operate(s, _):
                out = apply(s, lambda n: split_row(ext[pl.ds(n, 1), :]))
                mres[pl.ds(s, 1), :] = out[0:1] + out[1:2]
                return 0

            lax.fori_loop(0, S, operate, 0, unroll=8)
            src[...] = src[...] - (2.0 * step - mres[...] / ztot[...])
            rho_new = 1.0 / (2.0 * sigma - rho)
            step = rho_new * rho * step + 2.0 * rho_new / delta * precondition()
            rho = rho_new

    total_p[...] = step0[...] + step1[...] + step2[...]
    count = counts_ref[0, 0]
    live = lax.broadcasted_iota(jnp.int32, (S, T), 0) < count
    press_ref[0, 0] = jnp.where(live, total_p[0:S], 0.0)

    def gradient(s, _):
        def feature(n):
            return split(jnp.where(row4 == 3, 1.0, pos[n]) * total_p[pl.ds(n, 1), :])

        out = apply(s, feature)
        out = out[0:4] + out[4:8]
        known = sums[s]
        place = pos[s]
        own_p = total_p[pl.ds(s, 1), :]
        total = known[7:8]
        value = out - place * out[3:4] - own_p * known[0:4] + own_p * place * total
        result = flow[s] - 2.0 * (value / total)
        alive = jnp.full((3, T), count, jnp.int32) > s
        result = jnp.where(alive, result[0:3], 0.0)
        for c in range(3):
            vel_ref[0, 0, c, pl.ds(s, 1), :] = result[c:c + 1]
        return 0

    lax.fori_loop(0, S, gradient, 0, unroll=8)

    finish(0, pos, st_pos)
    finish(1, mot, st_mot)
    finish(2, flow, st_flow)
    finish(LATE, flow, st_late)
    for it in range(ITERS):
        finish(3 + it, steps[it], st_step[it])


def body(px, py, particles, dinv, low_bound, high_bound, counts, send_list, nbr_dir, nbr_slot):
    S, T = particles.shape[2], particles.shape[4]
    G = send_list.shape[2]
    K = nbr_dir.shape[3]
    N = S + 9 * G
    vmem = pl.BlockSpec(memory_space=pltpu.VMEM)
    smem = pl.BlockSpec(memory_space=pltpu.SMEM)
    exchanges = 4 + ITERS
    swap = lambda array: jnp.swapaxes(array, 2, 3)
    press, vel = pl.pallas_call(
        functools.partial(kernel, px, py, (S, G, K, T)),
        out_shape=(jax.ShapeDtypeStruct((1, 1, S, T), F32), jax.ShapeDtypeStruct((1, 1, 3, S, T), F32)),
        in_specs=[vmem, pl.BlockSpec(memory_space=pltpu.HBM), smem, smem, smem, smem, smem, smem],
        out_specs=(vmem, vmem),
        scratch_shapes=[
            pltpu.VMEM((S, 2 * K * T, T), BF16),
            pltpu.VMEM((S, T, T), F32),
            pltpu.VMEM((S, 2 * T, T), BF16),
            pltpu.VMEM((N, 4, T), F32),
            pltpu.VMEM((N, 4, T), F32),
            pltpu.VMEM((N, 4, T), F32),
            *[pltpu.VMEM((N, T), F32)] * ITERS,
            pltpu.VMEM((S, T), F32),
            pltpu.VMEM((N, T), F32),
            pltpu.VMEM((S, 8, T), F32),
            pltpu.VMEM((S, T), F32),
            pltpu.VMEM((S, T), F32),
            pltpu.VMEM((S, T), F32),
            pltpu.VMEM((G, 4, T), F32),
            pltpu.VMEM((G, 4, T), F32),
            pltpu.VMEM((G // 2, 4, T), F32),
            pltpu.VMEM((G - G // 2, 4, T), F32),
            *[pltpu.VMEM((G, T), F32)] * ITERS,
            pltpu.SemaphoreType.DMA,
            pltpu.SemaphoreType.DMA((exchanges, 9)),
            pltpu.SemaphoreType.DMA((exchanges, 9)),
        ],
        compiler_params=pltpu.CompilerParams(
            collective_id=0, has_side_effects=True, vmem_limit_bytes=48 << 20),
    )(swap(particles), dinv, low_bound, high_bound, counts, send_list, swap(nbr_dir), swap(nbr_slot))
    return press, swap(vel)


def solution(mesh):
    placed = (
        P("gx", "gy", None, None, None),
        P("gx", "gy", None, None, None),
        P(),
        P(),
        P("gx", "gy"),
        P("gx", "gy", None),
        P("gx", "gy", None, None),
        P("gx", "gy", None, None),
    )
    return jax.shard_map(
        functools.partial(body, mesh.shape["gx"], mesh.shape["gy"]),
        mesh=mesh,
        in_specs=placed,
        out_specs=(P("gx", "gy", None, None), P("gx", "gy", None, None, None)),
        check_vma=False,
    )
```
